32 devices in a mesh: ctx: 8 (over z, y), tp: 4 (over x, core).
Axes of the slice: x: 2, y: 2, z: 4, core: 2. Of those that a mesh axis runs over, the one named last changes fastest.
Arguments:
- query: bfloat16 [4096, 6144], P('ctx', 'tp'), may hold values from -6 to 6
- key_in: bfloat16 [4096, 6144], P('ctx', 'tp'), may hold values from -6 to 6
- value_in: bfloat16 [4096, 6144], P('ctx', 'tp'), may hold values from -6 to 6
- dout: bfloat16 [4096, 6144], P('ctx', 'tp'), may hold values from -0.5 to 0.5
- summary_offset: int32 [1], replicated, may hold values from 0 to 31
Outputs:
- grad_query: bfloat16 [4096, 6144], P(('ctx', 'tp'))
- grad_key: bfloat16 [4096, 6144], P(('ctx', 'tp'))
- grad_value: bfloat16 [4096, 6144], P(('ctx', 'tp'))
The draws below stay inside these ranges and needn't reach their ends.
Inputs may be any that keep to these rules, and one draw needn't show every extreme that they name: Summary block s is block s * 32 + summary_offset[s].
All inputs are finite; a program needn't handle non-finite values.
Results may differ from the reference program's by a relative error of at most 0.014.
Values may be sent and summed in bfloat16 or wider, within the bound.
A program may use at most 128 MiB of HBM per device.

```python
import jax
import jax.numpy as jnp
from jax import lax

HEADS = 48
HDIM = 128
BLOCK = 128
BAND = 8
STRIDE = 32
SEQ = 4096
NSUM = 1


def base_draw(key, salt):
    width = HEADS * HDIM
    values = jnp.clip(jax.random.normal(jax.random.fold_in(key, salt), (SEQ, width), jnp.float32), -6.0, 6.0)
    return values


def draw_query(key, part):
    values = base_draw(key, 11)
    return values.astype(jnp.bfloat16)


def draw_key_in(key, part):
    values = base_draw(key, 12)
    return values.astype(jnp.bfloat16)


def steps_of(stream_key, shape, split, low, largest):
    def one(position, shards_of):
        steps = jax.random.uniform(jax.random.fold_in(jax.random.fold_in(stream_key, 6), position), (shards_of,), jnp.float32, low / len(split), largest / len(split))
        return jnp.repeat(jnp.exp(steps), shape[position] // shards_of).reshape((-1,) + (1,) * (len(shape) - position - 1))

    gain = one(*split[0])
    for cut in split[1:]:
        gain = gain * one(*cut)
    return gain


def gaussian(rng, dims, deviation, reach, split=(), held_as=jnp.bfloat16):
    values = jax.random.normal(rng, dims, jnp.float32) * deviation
    if len(split) > 0:
        values = steps_of(rng, dims, split, -0.22, 0.18) * values
    return jnp.clip(values, min=-reach, max=reach).astype(held_as)


def setup_inputs(seed: int = 0) -> dict:
    key_of = jax.random.split(jax.random.key(seed), 6)
    return {
        "query": draw_query(jax.random.fold_in(key_of[5], 71), 0),
        "key_in": draw_key_in(jax.random.fold_in(key_of[5], 71), 0),
        "value_in": gaussian(key_of[2], (SEQ, HEADS * HDIM), 1.0, 6.0, ((0, 8), (1, 4))),
        "dout": gaussian(key_of[3], (SEQ, HEADS * HDIM), HDIM ** -0.5, 0.5, ((0, 8), (1, 4))),
        "summary_offset": jax.random.randint(key_of[4], (NSUM,), 0, STRIDE).astype(jnp.int32),
    }


def reference(query, key_in, value_in, dout, summary_offset):
    seq, width = query.shape
    heads = width // HDIM
    blocks = seq // BLOCK
    scale = HDIM ** -0.5
    groups = (jnp.arange(NSUM, dtype=jnp.int32) * STRIDE + summary_offset).astype(jnp.int32)
    key_blocks = key_in.reshape(blocks, BLOCK, width)
    value_blocks = value_in.reshape(blocks, BLOCK, width)
    within = jnp.arange(BLOCK, dtype=jnp.int32)
    nkeys = BAND + NSUM

    def step(carry, qblock):
        grad_k, grad_v = carry
        band = qblock - (BAND - 1) + jnp.arange(BAND, dtype=jnp.int32)
        valid = jnp.concatenate([band >= 0, groups < qblock - (BAND - 1)])
        index = jnp.concatenate([jnp.maximum(band, 0), groups]).astype(jnp.int32)
        keys = key_blocks[index].reshape(nkeys * BLOCK, heads, HDIM).astype(jnp.float32)
        values = value_blocks[index].reshape(nkeys * BLOCK, heads, HDIM).astype(jnp.float32)
        start = (qblock * BLOCK).astype(jnp.int32)
        rows_q = lax.dynamic_slice_in_dim(query, start, BLOCK, 0).reshape(BLOCK, heads, HDIM).astype(jnp.float32)
        rows_do = lax.dynamic_slice_in_dim(dout, start, BLOCK, 0).reshape(BLOCK, heads, HDIM).astype(jnp.float32)
        key_tok = (index[:, None] * BLOCK + within[None, :]).reshape(-1)
        query_tok = start + within
        allowed = jnp.repeat(valid, BLOCK)[None, :] & (key_tok[None, :] <= query_tok[:, None])
        allowed = allowed[None, :, :]
        scores = jnp.einsum("qhd,khd->hqk", rows_q, keys) * scale
        top = jnp.max(jnp.where(allowed, scores, -jnp.inf), axis=2, keepdims=True)
        total = jnp.sum(jnp.where(allowed, jnp.exp(scores - top), 0.0), axis=2, keepdims=True)
        lse = top + jnp.log(total)
        prob = jnp.where(allowed, jnp.exp(scores - lse), 0.0)
        dprob = jnp.einsum("qhd,khd->hqk", rows_do, values)
        delta = jnp.sum(prob * dprob, axis=2, keepdims=True)
        dscore = (prob * (dprob - delta)).astype(jnp.bfloat16).astype(jnp.float32)
        prob_low = prob.astype(jnp.bfloat16).astype(jnp.float32)
        grad_q = (jnp.einsum("hqk,khd->qhd", dscore, keys) * scale).astype(jnp.bfloat16)
        part_k = jnp.einsum("hqk,qhd->khd", dscore, rows_q) * scale
        part_v = jnp.einsum("hqk,qhd->khd", prob_low, rows_do)
        grad_k = grad_k.at[index].add(part_k.reshape(nkeys, BLOCK, width))
        grad_v = grad_v.at[index].add(part_v.reshape(nkeys, BLOCK, width))
        return (grad_k, grad_v), grad_q.reshape(BLOCK, width)

    empty = jnp.zeros((blocks, BLOCK, width), jnp.float32)
    (grad_k, grad_v), grad_q = lax.scan(step, (empty, empty), jnp.arange(blocks, dtype=jnp.int32))
    return (grad_q.reshape(seq, width), grad_k.reshape(seq, width).astype(jnp.bfloat16), grad_v.reshape(seq, width).astype(jnp.bfloat16))
```

```python
import functools
import math

import jax
import jax.numpy as jnp
from jax import lax
from jax.experimental import pallas as pl
from jax.experimental.pallas import tpu as pltpu
from jax.sharding import PartitionSpec as P

HDIM = 128
BLOCK = 128
BAND = 8
STRIDE = 32
REACH = 2
PAIR = 2 * BLOCK
CHUNKS = 3


def shifted(value, axis, steps):
    count = lax.axis_size(axis)
    leading, last = (max(0, -steps), min(count, count - steps))
    return lax.ppermute(value, axis, [(source, source + steps) for source in range(leading, last)])


def swapped(value, axis):
    count = lax.axis_size(axis)
    return lax.ppermute(value, axis, [(source, source ^ 1) for source in range(count)])


def attend(n_sum, info, q, do, kv2, kv1, kv0, kvs, gq, p2, p1, p0, ps):
    me = info[0]
    rows = q.shape[0]
    blocks = rows // BLOCK
    band = (BAND + 1) * BLOCK
    scale = HDIM ** (-0.5)
    key_at = lax.broadcasted_iota(jnp.int32, (band, PAIR), 0)
    query_at = lax.broadcasted_iota(jnp.int32, (1, PAIR), 1)
    last = query_at + (BAND - 1) * BLOCK
    second = query_at // BLOCK
    parts = []
    for pair in range(rows // PAIR):
        low = REACH * blocks + 2 * pair - (BAND - 1)
        pieces = []
        for index, ref in enumerate((kv2, kv1, kv0)):
            start = max(low - index * blocks, 0) * BLOCK
            stop = min(low + BAND + 1 - index * blocks, blocks) * BLOCK
            pieces.append((ref, start, stop))
        keys = jnp.concatenate([r[0, a:b] for r, a, b in pieces] + [kvs[0]], axis=0)
        values = jnp.concatenate([r[1, a:b] for r, a, b in pieces] + [kvs[1]], axis=0)
        span = slice(pair * PAIR, (pair + 1) * PAIR)
        rows_q = q[span]
        rows_do = do[span]
        scores = lax.dot_general(
            keys, rows_q, (((1,), (1,)), ((), ())), preferred_element_type=jnp.float32
        )
        first = jnp.maximum(second, (REACH - me) * blocks - low) * BLOCK
        ok = (key_at >= first) & (key_at <= last)
        masked = [jnp.where(ok, scores[:band], -jnp.inf)]
        query_block = me * blocks + 2 * pair + second
        for s in range(n_sum):
            ok_s = info[1 + s] < query_block - (BAND - 1)
            tile = scores[band + s * BLOCK : band + (s + 1) * BLOCK]
            masked.append(jnp.where(ok_s, tile, -jnp.inf))
        scores = jnp.concatenate(masked, axis=0)
        top = jnp.max(scores, axis=0, keepdims=True)
        raw = jnp.exp2((scores - top) * (scale * math.log2(math.e)))
        inverse = 1.0 / jnp.sum(raw, axis=0, keepdims=True)
        prob = raw * inverse
        dprob = lax.dot_general(
            values, rows_do, (((1,), (1,)), ((), ())), preferred_element_type=jnp.float32
        )
        delta = jnp.sum(prob * dprob, axis=0, keepdims=True)
        dscore = (prob * (dprob - delta)).astype(jnp.bfloat16)
        prob_low = prob.astype(jnp.bfloat16)
        part_v = jnp.dot(prob_low, rows_do, preferred_element_type=jnp.float32)
        part_k = jnp.dot(dscore, rows_q, preferred_element_type=jnp.float32) * scale
        grad_q = lax.dot_general(
            keys, dscore, (((0,), (0,)), ((), ())), preferred_element_type=jnp.float32
        )
        gq[span] = (grad_q * scale).T.astype(gq.dtype)
        parts.append((low, part_k, part_v))
    for index, out in enumerate((p2, p1, p0)):
        for which in range(2):
            for block in range(blocks):
                total = None
                for part in parts:
                    at = index * blocks + block - part[0]
                    if 0 <= at <= BAND:
                        piece = part[1 + which][at * BLOCK : (at + 1) * BLOCK]
                        total = piece if total is None else total + piece
                if total is None:
                    total = jnp.zeros((BLOCK, HDIM), jnp.float32)
                out[which, block * BLOCK : (block + 1) * BLOCK] = total.astype(out.dtype)
    for which in range(2):
        total = parts[0][1 + which][band:]
        for part in parts[1:]:
            total = total + part[1 + which][band:]
        ps[which] = total


def attention(info, query, dout, kv2, kv1, kv0, kvs, first_head, n_sum):
    rows = query.shape[0]
    width = kv0.shape[2]
    heads = width // HDIM
    mine = pl.BlockSpec((rows, HDIM), lambda h: (0, first_head + h))
    wide = pl.BlockSpec((2, rows, HDIM), lambda h: (0, 0, h))
    tile = pl.BlockSpec((2, n_sum * BLOCK, HDIM), lambda h: (0, 0, h))
    pairs = rows // PAIR * (BAND + 1 + n_sum) * BLOCK * PAIR
    return pl.pallas_call(
        functools.partial(attend, n_sum),
        grid=(heads,),
        in_specs=[pl.BlockSpec(memory_space=pltpu.SMEM), mine, mine, wide, wide, wide, tile],
        out_specs=[
            pl.BlockSpec((rows, HDIM), lambda h: (0, h)),
            wide,
            wide,
            wide,
            tile,
        ],
        out_shape=[
            jax.ShapeDtypeStruct((rows, width), jnp.bfloat16),
            jax.ShapeDtypeStruct((2, rows, width), jnp.bfloat16),
            jax.ShapeDtypeStruct((2, rows, width), jnp.bfloat16),
            jax.ShapeDtypeStruct((2, rows, width), jnp.float32),
            jax.ShapeDtypeStruct((2, n_sum * BLOCK, width), jnp.float32),
        ],
        compiler_params=pltpu.CompilerParams(vmem_limit_bytes=40 * 1024 * 1024),
        cost_estimate=pl.CostEstimate(
            flops=heads * pairs * 10 * HDIM,
            bytes_accessed=heads * rows * HDIM * 32,
            transcendentals=heads * pairs,
        ),
    )(info, query, dout, kv2, kv1, kv0, kvs)


def on_device(query, key_in, value_in, dout, summary_offset):
    rows, width = query.shape
    me = lax.axis_index("ctx")
    n_ctx = lax.axis_size("ctx")
    n_tp = lax.axis_size("tp")
    n_sum = summary_offset.shape[0]
    groups = jnp.arange(n_sum, dtype=jnp.int32) * STRIDE + summary_offset
    owner = groups * BLOCK // rows
    local_start = groups * BLOCK - owner * rows
    distance = me - owner
    tile_distance = jnp.repeat(distance, BLOCK)[None, :, None]
    info = jnp.concatenate([me.astype(jnp.int32)[None], groups])
    odd = me % 2 == 1
    jumps = []
    reached = REACH + 1
    while reached < n_ctx:
        jumps.append(reached)
        reached *= 2
    part = width // CHUNKS
    heads = part // HDIM

    ready = []
    for chunk in range(CHUNKS):
        span = slice(chunk * part, (chunk + 1) * part)
        kv0 = jnp.stack([key_in[:, span], value_in[:, span]])
        kv2 = shifted(kv0, "ctx", 2)
        kv1 = swapped(jnp.where(odd, kv2, kv0), "ctx")
        tiles = []
        for s in range(n_sum):
            at = (0, local_start[s], 0)
            size = (2, BLOCK, part)
            far = lax.dynamic_slice(kv2, at, size)
            near = lax.dynamic_slice(kv1, at, size)
            own = lax.dynamic_slice(kv0, at, size)
            tiles.append(
                jnp.where(distance[s] == 2, far, jnp.where(distance[s] == 1, near, own))
            )
        kvs = jnp.concatenate(tiles, axis=1)
        for jump in jumps:
            got = shifted(kvs, "ctx", jump)
            kvs = jnp.where((tile_distance >= jump) & (tile_distance < 2 * jump), got, kvs)
        ready.append((kv2, kv1, kv0, kvs))

    grads = []
    for chunk in range(CHUNKS):
        gq, p2, p1, p0, ps = attention(
            info, query, dout, *ready[chunk], chunk * heads, n_sum
        )
        moved_q = lax.all_to_all(gq, "tp", split_axis=0, concat_axis=1, tiled=True)
        for jump in reversed(jumps):
            got = shifted(ps.astype(jnp.bfloat16), "ctx", -jump).astype(jnp.float32)
            ps = jnp.where((tile_distance >= 0) & (tile_distance < jump), ps + got, ps)

        def add_tile(array, s, away):
            at = (0, local_start[s], 0)
            piece = lax.dynamic_slice(array, at, (2, BLOCK, part)).astype(jnp.float32)
            term = jnp.where(distance[s] == away, ps[:, s * BLOCK : (s + 1) * BLOCK], 0.0)
            return lax.dynamic_update_slice(array, (piece + term).astype(array.dtype), at)

        for s in range(n_sum):
            p2 = add_tile(p2, s, 2)
            p1 = add_tile(p1, s, 1)
            p0 = add_tile(p0, s, 0)
        near = swapped(p1, "ctx").astype(jnp.float32)
        p2 = jnp.where(odd, p2.astype(jnp.float32) + near, p2.astype(jnp.float32))
        far = shifted(p2.astype(jnp.bfloat16), "ctx", -2).astype(jnp.float32)
        total = (p0 + jnp.where(odd, 0.0, near) + far).astype(jnp.bfloat16)
        moved_kv = lax.all_to_all(total, "tp", split_axis=1, concat_axis=2, tiled=True)
        grads.append((moved_q, moved_kv[0], moved_kv[1]))

    def joined(pieces):
        split = [piece.reshape(rows // n_tp, n_tp, part) for piece in pieces]
        return jnp.concatenate(split, axis=2).reshape(rows // n_tp, n_tp * width)

    return tuple(joined([grad[which] for grad in grads]) for which in range(3))


def solution(mesh):
    return jax.shard_map(
        on_device,
        mesh=mesh,
        in_specs=(P("ctx", "tp"), P("ctx", "tp"), P("ctx", "tp"), P("ctx", "tp"), P()),
        out_specs=(P(("ctx", "tp"), None), P(("ctx", "tp"), None), P(("ctx", "tp"), None)),
        check_vma=False,
    )
```

```python
import functools
import math

import jax
import jax.numpy as jnp
from jax import lax
from jax.experimental import pallas as pl
from jax.experimental.pallas import tpu as pltpu
from jax.sharding import PartitionSpec as P

HDIM = 128
BLOCK = 128
BAND = 8
STRIDE = 32
REACH = 2
PAIR = 2 * BLOCK
CHUNKS = 3


def shifted(value, axis, steps):
    count = lax.axis_size(axis)
    leading, last = (max(0, -steps), min(count, count - steps))
    return lax.ppermute(value, axis, [(source, source + steps) for source in range(leading, last)])


def swapped(value, axis):
    count = lax.axis_size(axis)
    return lax.ppermute(value, axis, [(source, source ^ 1) for source in range(count)])


def attend(n_sum, info, q, do, kv2, kv1, kv0, kvs, after, gq, p2, p1, p0, ps, token):
    me = info[0]
    token[0] = me
    rows = q.shape[0]
    blocks = rows // BLOCK
    band = (BAND + 1) * BLOCK
    scale = HDIM ** (-0.5)
    key_at = lax.broadcasted_iota(jnp.int32, (band, PAIR), 0)
    query_at = lax.broadcasted_iota(jnp.int32, (1, PAIR), 1)
    last = query_at + (BAND - 1) * BLOCK
    second = query_at // BLOCK
    parts = []
    for pair in range(rows // PAIR):
        low = REACH * blocks + 2 * pair - (BAND - 1)
        pieces = []
        for index, ref in enumerate((kv2, kv1, kv0)):
            start = max(low - index * blocks, 0) * BLOCK
            stop = min(low + BAND + 1 - index * blocks, blocks) * BLOCK
            pieces.append((ref, start, stop))
        keys = jnp.concatenate([r[0, a:b] for r, a, b in pieces] + [kvs[0]], axis=0)
        values = jnp.concatenate([r[1, a:b] for r, a, b in pieces] + [kvs[1]], axis=0)
        span = slice(pair * PAIR, (pair + 1) * PAIR)
        rows_q = q[span]
        rows_do = do[span]
        scores = lax.dot_general(
            keys, rows_q, (((1,), (1,)), ((), ())), preferred_element_type=jnp.float32
        )
        first = jnp.maximum(second, (REACH - me) * blocks - low) * BLOCK
        ok = (key_at >= first) & (key_at <= last)
        masked = [jnp.where(ok, scores[:band], -jnp.inf)]
        query_block = me * blocks + 2 * pair + second
        for s in range(n_sum):
            ok_s = info[1 + s] < query_block - (BAND - 1)
            tile = scores[band + s * BLOCK : band + (s + 1) * BLOCK]
            masked.append(jnp.where(ok_s, tile, -jnp.inf))
        scores = jnp.concatenate(masked, axis=0)
        top = jnp.max(scores, axis=0, keepdims=True)
        raw = jnp.exp2((scores - top) * (scale * math.log2(math.e)))
        inverse = 1.0 / jnp.sum(raw, axis=0, keepdims=True)
        prob = raw * inverse
        dprob = lax.dot_general(
            values, rows_do, (((1,), (1,)), ((), ())), preferred_element_type=jnp.float32
        )
        delta = jnp.sum(prob * dprob, axis=0, keepdims=True)
        dscore = (prob * (dprob - delta)).astype(jnp.bfloat16)
        prob_low = prob.astype(jnp.bfloat16)
        part_v = jnp.dot(prob_low, rows_do, preferred_element_type=jnp.float32)
        part_k = jnp.dot(dscore, rows_q, preferred_element_type=jnp.float32) * scale
        grad_q = lax.dot_general(
            keys, dscore, (((0,), (0,)), ((), ())), preferred_element_type=jnp.float32
        )
        gq[span] = (grad_q * scale).T.astype(gq.dtype)
        parts.append((low, part_k, part_v))
    for index, out in enumerate((p2, p1, p0)):
        for which in range(2):
            for block in range(blocks):
                total = None
                for part in parts:
                    at = index * blocks + block - part[0]
                    if 0 <= at <= BAND:
                        piece = part[1 + which][at * BLOCK : (at + 1) * BLOCK]
                        total = piece if total is None else total + piece
                if total is None:
                    total = jnp.zeros((BLOCK, HDIM), jnp.float32)
                out[which, block * BLOCK : (block + 1) * BLOCK] = total.astype(out.dtype)
    for which in range(2):
        total = parts[0][1 + which][band:]
        for part in parts[1:]:
            total = total + part[1 + which][band:]
        ps[which] = total


def attention(info, query, dout, kv2, kv1, kv0, kvs, after, first_head, n_sum):
    rows = query.shape[0]
    width = kv0.shape[2]
    heads = width // HDIM
    mine = pl.BlockSpec((rows, HDIM), lambda h: (0, first_head + h))
    wide = pl.BlockSpec((2, rows, HDIM), lambda h: (0, 0, h))
    tile = pl.BlockSpec((2, n_sum * BLOCK, HDIM), lambda h: (0, 0, h))
    pairs = rows // PAIR * (BAND + 1 + n_sum) * BLOCK * PAIR
    return pl.pallas_call(
        functools.partial(attend, n_sum),
        grid=(heads,),
        in_specs=[
            pl.BlockSpec(memory_space=pltpu.SMEM),
            mine,
            mine,
            wide,
            wide,
            wide,
            tile,
            pl.BlockSpec(memory_space=pl.ANY),
        ],
        out_specs=[
            pl.BlockSpec((rows, HDIM), lambda h: (0, h)),
            wide,
            wide,
            wide,
            tile,
            pl.BlockSpec(memory_space=pltpu.SMEM),
        ],
        out_shape=[
            jax.ShapeDtypeStruct((rows, width), jnp.bfloat16),
            jax.ShapeDtypeStruct((2, rows, width), jnp.bfloat16),
            jax.ShapeDtypeStruct((2, rows, width), jnp.bfloat16),
            jax.ShapeDtypeStruct((2, rows, width), jnp.float32),
            jax.ShapeDtypeStruct((2, n_sum * BLOCK, width), jnp.float32),
            jax.ShapeDtypeStruct((1,), jnp.int32),
        ],
        compiler_params=pltpu.CompilerParams(vmem_limit_bytes=40 * 1024 * 1024),
        cost_estimate=pl.CostEstimate(
            flops=heads * pairs * 10 * HDIM,
            bytes_accessed=heads * rows * HDIM * 32,
            transcendentals=heads * pairs,
        ),
    )(info, query, dout, kv2, kv1, kv0, kvs, after)


def on_device(query, key_in, value_in, dout, summary_offset):
    rows, width = query.shape
    me = lax.axis_index("ctx")
    n_ctx = lax.axis_size("ctx")
    n_tp = lax.axis_size("tp")
    n_sum = summary_offset.shape[0]
    groups = jnp.arange(n_sum, dtype=jnp.int32) * STRIDE + summary_offset
    owner = groups * BLOCK // rows
    local_start = groups * BLOCK - owner * rows
    distance = me - owner
    tile_distance = jnp.repeat(distance, BLOCK)[None, :, None]
    info = jnp.concatenate([me.astype(jnp.int32)[None], groups])
    odd = me % 2 == 1
    jumps = []
    reached = REACH + 1
    while reached < n_ctx:
        jumps.append(reached)
        reached *= 2
    part = width // CHUNKS
    heads = part // HDIM

    stacked = []
    for chunk in range(CHUNKS):
        span = slice(chunk * part, (chunk + 1) * part)
        kv0 = jnp.stack([key_in[:, span], value_in[:, span]])
        stacked.append((kv0, shifted(kv0, "ctx", 2)))

    def gathered(kv0, kv2, here):
        kv1 = swapped(jnp.where(here % 2 == 1, kv2, kv0), "ctx")
        tiles = []
        for s in range(n_sum):
            at = (0, local_start[s], 0)
            size = (2, BLOCK, part)
            far = lax.dynamic_slice(kv2, at, size)
            near = lax.dynamic_slice(kv1, at, size)
            own = lax.dynamic_slice(kv0, at, size)
            tiles.append(
                jnp.where(distance[s] == 2, far, jnp.where(distance[s] == 1, near, own))
            )
        kvs = jnp.concatenate(tiles, axis=1)
        for jump in jumps:
            got = shifted(kvs, "ctx", jump)
            kvs = jnp.where((tile_distance >= jump) & (tile_distance < 2 * jump), got, kvs)
        return kv2, kv1, kv0, kvs

    def returned(p2, p1, p0, ps):
        for jump in reversed(jumps):
            got = shifted(ps.astype(jnp.bfloat16), "ctx", -jump).astype(jnp.float32)
            ps = jnp.where((tile_distance >= 0) & (tile_distance < jump), ps + got, ps)

        def add_tile(array, s, away):
            at = (0, local_start[s], 0)
            piece = lax.dynamic_slice(array, at, (2, BLOCK, part)).astype(jnp.float32)
            term = jnp.where(distance[s] == away, ps[:, s * BLOCK : (s + 1) * BLOCK], 0.0)
            return lax.dynamic_update_slice(array, (piece + term).astype(array.dtype), at)

        for s in range(n_sum):
            p2 = add_tile(p2, s, 2)
            p1 = add_tile(p1, s, 1)
            p0 = add_tile(p0, s, 0)
        near = swapped(p1, "ctx")
        wide = near.astype(jnp.float32)
        p2 = jnp.where(odd, p2.astype(jnp.float32) + wide, p2.astype(jnp.float32))
        far = shifted(p2.astype(jnp.bfloat16), "ctx", -2).astype(jnp.float32)
        total = (p0 + jnp.where(odd, 0.0, wide) + far).astype(jnp.bfloat16)
        return near, lax.all_to_all(total, "tp", split_axis=1, concat_axis=2, tiled=True)

    grads = []
    tokens = []
    returns = []
    for chunk in range(CHUNKS):
        here = tokens[chunk - 2][0] if chunk >= 2 else me
        after = returns[chunk - 2] if chunk >= 2 else summary_offset
        ready = gathered(*stacked[chunk], here)
        gq, p2, p1, p0, ps, token = attention(
            info, query, dout, *ready, after, chunk * heads, n_sum
        )
        tokens.append(token)
        moved_q = lax.all_to_all(gq, "tp", split_axis=0, concat_axis=1, tiled=True)
        near, moved_kv = returned(p2, p1, p0, ps)
        returns.append(near)
        grads.append((moved_q, moved_kv[0], moved_kv[1]))

    def joined(pieces):
        split = [piece.reshape(rows // n_tp, n_tp, part) for piece in pieces]
        return jnp.concatenate(split, axis=2).reshape(rows // n_tp, n_tp * width)

    return tuple(joined([grad[which] for grad in grads]) for which in range(3))


def solution(mesh):
    return jax.shard_map(
        on_device,
        mesh=mesh,
        in_specs=(P("ctx", "tp"), P("ctx", "tp"), P("ctx", "tp"), P("ctx", "tp"), P()),
        out_specs=(P(("ctx", "tp"), None), P(("ctx", "tp"), None), P(("ctx", "tp"), None)),
        check_vma=False,
    )
```

```python
import functools
import math

import jax
import jax.numpy as jnp
from jax import lax
from jax.experimental import pallas as pl
from jax.experimental.pallas import tpu as pltpu
from jax.sharding import PartitionSpec as P

HDIM = 128
BLOCK = 128
BAND = 8
STRIDE = 32
REACH = 2
PAIR = 2 * BLOCK
CHUNKS = 2


def shifted(value, axis, steps):
    count = lax.axis_size(axis)
    leading, last = (max(0, -steps), min(count, count - steps))
    return lax.ppermute(value, axis, [(source, source + steps) for source in range(leading, last)])


def swapped(value, axis):
    count = lax.axis_size(axis)
    return lax.ppermute(value, axis, [(source, source ^ 1) for source in range(count)])


def attend(n_sum, info, q, do, kv2, kv1, kv0, kvs, after, gq, p2, p1, p0, ps, token):
    me = info[0]
    token[0] = me
    rows = q.shape[0]
    blocks = rows // BLOCK
    band = (BAND + 1) * BLOCK
    scale = HDIM ** (-0.5)
    key_at = lax.broadcasted_iota(jnp.int32, (band, PAIR), 0)
    query_at = lax.broadcasted_iota(jnp.int32, (1, PAIR), 1)
    last = query_at + (BAND - 1) * BLOCK
    second = query_at // BLOCK
    parts = []
    for pair in range(rows // PAIR):
        low = REACH * blocks + 2 * pair - (BAND - 1)
        pieces = []
        for index, ref in enumerate((kv2, kv1, kv0)):
            start = max(low - index * blocks, 0) * BLOCK
            stop = min(low + BAND + 1 - index * blocks, blocks) * BLOCK
            pieces.append((ref, start, stop))
        keys = jnp.concatenate([r[0, a:b] for r, a, b in pieces] + [kvs[0]], axis=0)
        values = jnp.concatenate([r[1, a:b] for r, a, b in pieces] + [kvs[1]], axis=0)
        span = slice(pair * PAIR, (pair + 1) * PAIR)
        rows_q = q[span]
        rows_do = do[span]
        scores = lax.dot_general(
            keys, rows_q, (((1,), (1,)), ((), ())), preferred_element_type=jnp.float32
        )
        first = jnp.maximum(second, (REACH - me) * blocks - low) * BLOCK
        ok = (key_at >= first) & (key_at <= last)
        masked = [jnp.where(ok, scores[:band], -jnp.inf)]
        query_block = me * blocks + 2 * pair + second
        for s in range(n_sum):
            ok_s = info[1 + s] < query_block - (BAND - 1)
            tile = scores[band + s * BLOCK : band + (s + 1) * BLOCK]
            masked.append(jnp.where(ok_s, tile, -jnp.inf))
        scores = jnp.concatenate(masked, axis=0)
        top = jnp.max(scores, axis=0, keepdims=True)
        raw = jnp.exp2((scores - top) * (scale * math.log2(math.e)))
        inverse = 1.0 / jnp.sum(raw, axis=0, keepdims=True)
        prob = raw * inverse
        dprob = lax.dot_general(
            values, rows_do, (((1,), (1,)), ((), ())), preferred_element_type=jnp.float32
        )
        delta = jnp.sum(prob * dprob, axis=0, keepdims=True)
        dscore = (prob * (dprob - delta)).astype(jnp.bfloat16)
        prob_low = prob.astype(jnp.bfloat16)
        part_v = jnp.dot(prob_low, rows_do, preferred_element_type=jnp.float32)
        part_k = jnp.dot(dscore, rows_q, preferred_element_type=jnp.float32) * scale
        grad_q = lax.dot_general(
            keys, dscore, (((0,), (0,)), ((), ())), preferred_element_type=jnp.float32
        )
        gq[span] = (grad_q * scale).T.astype(gq.dtype)
        parts.append((low, part_k, part_v))
    for index, out in enumerate((p2, p1, p0)):
        for which in range(2):
            for block in range(blocks):
                total = None
                for part in parts:
                    at = index * blocks + block - part[0]
                    if 0 <= at <= BAND:
                        piece = part[1 + which][at * BLOCK : (at + 1) * BLOCK]
                        total = piece if total is None else total + piece
                if total is None:
                    total = jnp.zeros((BLOCK, HDIM), jnp.float32)
                out[which, block * BLOCK : (block + 1) * BLOCK] = total.astype(out.dtype)
    for which in range(2):
        total = parts[0][1 + which][band:]
        for part in parts[1:]:
            total = total + part[1 + which][band:]
        ps[which] = total


def attention(info, query, dout, kv2, kv1, kv0, kvs, after, first_head, n_sum):
    rows = query.shape[0]
    width = kv0.shape[2]
    heads = width // HDIM
    mine = pl.BlockSpec((rows, HDIM), lambda h: (0, first_head + h))
    wide = pl.BlockSpec((2, rows, HDIM), lambda h: (0, 0, h))
    tile = pl.BlockSpec((2, n_sum * BLOCK, HDIM), lambda h: (0, 0, h))
    pairs = rows // PAIR * (BAND + 1 + n_sum) * BLOCK * PAIR
    return pl.pallas_call(
        functools.partial(attend, n_sum),
        grid=(heads,),
        in_specs=[
            pl.BlockSpec(memory_space=pltpu.SMEM),
            mine,
            mine,
            wide,
            wide,
            wide,
            tile,
            pl.BlockSpec(memory_space=pl.ANY),
        ],
        out_specs=[
            pl.BlockSpec((rows, HDIM), lambda h: (0, h)),
            wide,
            wide,
            wide,
            tile,
            pl.BlockSpec(memory_space=pltpu.SMEM),
        ],
        out_shape=[
            jax.ShapeDtypeStruct((rows, width), jnp.bfloat16),
            jax.ShapeDtypeStruct((2, rows, width), jnp.bfloat16),
            jax.ShapeDtypeStruct((2, rows, width), jnp.bfloat16),
            jax.ShapeDtypeStruct((2, rows, width), jnp.float32),
            jax.ShapeDtypeStruct((2, n_sum * BLOCK, width), jnp.float32),
            jax.ShapeDtypeStruct((1,), jnp.int32),
        ],
        compiler_params=pltpu.CompilerParams(vmem_limit_bytes=40 * 1024 * 1024),
        cost_estimate=pl.CostEstimate(
            flops=heads * pairs * 10 * HDIM,
            bytes_accessed=heads * rows * HDIM * 32,
            transcendentals=heads * pairs,
        ),
    )(info, query, dout, kv2, kv1, kv0, kvs, after)


def on_device(query, key_in, value_in, dout, summary_offset):
    rows, width = query.shape
    me = lax.axis_index("ctx")
    n_ctx = lax.axis_size("ctx")
    n_tp = lax.axis_size("tp")
    n_sum = summary_offset.shape[0]
    groups = jnp.arange(n_sum, dtype=jnp.int32) * STRIDE + summary_offset
    owner = groups * BLOCK // rows
    local_start = groups * BLOCK - owner * rows
    distance = me - owner
    tile_distance = jnp.repeat(distance, BLOCK)[None, :, None]
    info = jnp.concatenate([me.astype(jnp.int32)[None], groups])
    odd = me % 2 == 1
    jumps = []
    reached = REACH + 1
    while reached < n_ctx:
        jumps.append(reached)
        reached *= 2
    part = width // CHUNKS
    heads = part // HDIM

    stacked = []
    for chunk in range(CHUNKS):
        span = slice(chunk * part, (chunk + 1) * part)
        kv0 = jnp.stack([key_in[:, span], value_in[:, span]])
        stacked.append((kv0, shifted(kv0, "ctx", 2)))

    def gathered(kv0, kv2, here):
        kv1 = swapped(jnp.where(odd, kv2, kv0), "ctx")
        away = here - owner
        tiles = []
        for s in range(n_sum):
            at = (0, local_start[s], 0)
            size = (2, BLOCK, part)
            far = lax.dynamic_slice(kv2, at, size)
            near = lax.dynamic_slice(kv1, at, size)
            own = lax.dynamic_slice(kv0, at, size)
            tiles.append(
                jnp.where(away[s] == 2, far, jnp.where(away[s] == 1, near, own))
            )
        kvs = jnp.concatenate(tiles, axis=1)
        for jump in jumps:
            got = shifted(kvs, "ctx", jump)
            kvs = jnp.where((tile_distance >= jump) & (tile_distance < 2 * jump), got, kvs)
        return kv2, kv1, kv0, kvs

    def returned(p2, p1, p0, ps):
        for jump in reversed(jumps):
            got = shifted(ps.astype(jnp.bfloat16), "ctx", -jump).astype(jnp.float32)
            ps = jnp.where((tile_distance >= 0) & (tile_distance < jump), ps + got, ps)

        def add_tile(array, s, away):
            at = (0, local_start[s], 0)
            piece = lax.dynamic_slice(array, at, (2, BLOCK, part)).astype(jnp.float32)
            term = jnp.where(distance[s] == away, ps[:, s * BLOCK : (s + 1) * BLOCK], 0.0)
            return lax.dynamic_update_slice(array, (piece + term).astype(array.dtype), at)

        for s in range(n_sum):
            p2 = add_tile(p2, s, 2)
            p1 = add_tile(p1, s, 1)
            p0 = add_tile(p0, s, 0)
        near = swapped(p1, "ctx")
        wide = near.astype(jnp.float32)
        p2 = jnp.where(odd, p2.astype(jnp.float32) + wide, p2.astype(jnp.float32))
        far = shifted(p2.astype(jnp.bfloat16), "ctx", -2).astype(jnp.float32)
        total = (p0 + jnp.where(odd, 0.0, wide) + far).astype(jnp.bfloat16)
        return ps, lax.all_to_all(total, "tp", split_axis=1, concat_axis=2, tiled=True)

    grads = []
    tokens = []
    returns = []
    for chunk in range(CHUNKS):
        here = tokens[chunk - 1][0] if chunk >= 1 else me
        after = returns[chunk - 1] if chunk >= 1 else summary_offset
        ready = gathered(*stacked[chunk], here)
        gq, p2, p1, p0, ps, token = attention(
            info, query, dout, *ready, after, chunk * heads, n_sum
        )
        tokens.append(token)
        moved_q = lax.all_to_all(gq, "tp", split_axis=0, concat_axis=1, tiled=True)
        summed, moved_kv = returned(p2, p1, p0, ps)
        returns.append(summed)
        grads.append((moved_q, moved_kv[0], moved_kv[1]))

    def joined(pieces):
        split = [piece.reshape(rows // n_tp, n_tp, part) for piece in pieces]
        return jnp.concatenate(split, axis=2).reshape(rows // n_tp, n_tp * width)

    return tuple(joined([grad[which] for grad in grads]) for which in range(3))


def solution(mesh):
    return jax.shard_map(
        on_device,
        mesh=mesh,
        in_specs=(P("ctx", "tp"), P("ctx", "tp"), P("ctx", "tp"), P("ctx", "tp"), P()),
        out_specs=(P(("ctx", "tp"), None), P(("ctx", "tp"), None), P(("ctx", "tp"), None)),
        check_vma=False,
    )
```

```python
import functools
import math

import jax
import jax.numpy as jnp
from jax import lax
from jax.experimental import pallas as pl
from jax.experimental.pallas import tpu as pltpu
from jax.sharding import PartitionSpec as P

HDIM = 128
BLOCK = 128
BAND = 8
STRIDE = 32
REACH = 2
PAIR = 2 * BLOCK
CHUNKS = 3


def shifted(value, axis, steps):
    count = lax.axis_size(axis)
    leading, last = (max(0, -steps), min(count, count - steps))
    return lax.ppermute(value, axis, [(source, source + steps) for source in range(leading, last)])


def swapped(value, axis):
    count = lax.axis_size(axis)
    return lax.ppermute(value, axis, [(source, source ^ 1) for source in range(count)])


def attend(n_sum, info, q, do, kv2, kv1, kv0, kvs, after, gq, p2, p1, p0, ps, token):
    me = info[0]
    token[0] = me
    rows = q.shape[0]
    blocks = rows // BLOCK
    band = (BAND + 1) * BLOCK
    scale = HDIM ** (-0.5)
    key_at = lax.broadcasted_iota(jnp.int32, (band, PAIR), 0)
    query_at = lax.broadcasted_iota(jnp.int32, (1, PAIR), 1)
    last = query_at + (BAND - 1) * BLOCK
    second = query_at // BLOCK
    parts = []
    for pair in range(rows // PAIR):
        low = REACH * blocks + 2 * pair - (BAND - 1)
        pieces = []
        for index, ref in enumerate((kv2, kv1, kv0)):
            start = max(low - index * blocks, 0) * BLOCK
            stop = min(low + BAND + 1 - index * blocks, blocks) * BLOCK
            pieces.append((ref, start, stop))
        keys = jnp.concatenate([r[0, a:b] for r, a, b in pieces] + [kvs[0]], axis=0)
        values = jnp.concatenate([r[1, a:b] for r, a, b in pieces] + [kvs[1]], axis=0)
        span = slice(pair * PAIR, (pair + 1) * PAIR)
        rows_q = q[span]
        rows_do = do[span]
        scores = lax.dot_general(
            keys, rows_q, (((1,), (1,)), ((), ())), preferred_element_type=jnp.float32
        )
        first = jnp.maximum(second, (REACH - me) * blocks - low) * BLOCK
        ok = (key_at >= first) & (key_at <= last)
        masked = [jnp.where(ok, scores[:band], -jnp.inf)]
        query_block = me * blocks + 2 * pair + second
        for s in range(n_sum):
            ok_s = info[1 + s] < query_block - (BAND - 1)
            tile = scores[band + s * BLOCK : band + (s + 1) * BLOCK]
            masked.append(jnp.where(ok_s, tile, -jnp.inf))
        scores = jnp.concatenate(masked, axis=0)
        top = jnp.max(scores, axis=0, keepdims=True)
        raw = jnp.exp2((scores - top) * (scale * math.log2(math.e)))
        inverse = 1.0 / jnp.sum(raw, axis=0, keepdims=True)
        prob = raw * inverse
        dprob = lax.dot_general(
            values, rows_do, (((1,), (1,)), ((), ())), preferred_element_type=jnp.float32
        )
        delta = jnp.sum(prob * dprob, axis=0, keepdims=True)
        dscore = (prob * (dprob - delta)).astype(jnp.bfloat16)
        prob_low = prob.astype(jnp.bfloat16)
        part_v = jnp.dot(prob_low, rows_do, preferred_element_type=jnp.float32)
        part_k = jnp.dot(dscore, rows_q, preferred_element_type=jnp.float32) * scale
        grad_q = lax.dot_general(
            keys, dscore, (((0,), (0,)), ((), ())), preferred_element_type=jnp.float32
        )
        gq[span] = (grad_q * scale).T.astype(gq.dtype)
        parts.append((low, part_k, part_v))
    for index, out in enumerate((p2, p1, p0)):
        for which in range(2):
            for block in range(blocks):
                total = None
                for part in parts:
                    at = index * blocks + block - part[0]
                    if 0 <= at <= BAND:
                        piece = part[1 + which][at * BLOCK : (at + 1) * BLOCK]
                        total = piece if total is None else total + piece
                if total is None:
                    total = jnp.zeros((BLOCK, HDIM), jnp.float32)
                out[which, block * BLOCK : (block + 1) * BLOCK] = total.astype(out.dtype)
    for which in range(2):
        total = parts[0][1 + which][band:]
        for part in parts[1:]:
            total = total + part[1 + which][band:]
        ps[which] = total


def attention(info, query, dout, kv2, kv1, kv0, kvs, after, first_head, n_sum):
    rows = query.shape[0]
    width = kv0.shape[2]
    heads = width // HDIM
    mine = pl.BlockSpec((rows, HDIM), lambda h: (0, first_head + h))
    wide = pl.BlockSpec((2, rows, HDIM), lambda h: (0, 0, h))
    tile = pl.BlockSpec((2, n_sum * BLOCK, HDIM), lambda h: (0, 0, h))
    pairs = rows // PAIR * (BAND + 1 + n_sum) * BLOCK * PAIR
    return pl.pallas_call(
        functools.partial(attend, n_sum),
        grid=(heads,),
        in_specs=[
            pl.BlockSpec(memory_space=pltpu.SMEM),
            mine,
            mine,
            wide,
            wide,
            wide,
            tile,
            pl.BlockSpec(memory_space=pl.ANY),
        ],
        out_specs=[
            pl.BlockSpec((rows, HDIM), lambda h: (0, h)),
            wide,
            wide,
            wide,
            tile,
            pl.BlockSpec(memory_space=pltpu.SMEM),
        ],
        out_shape=[
            jax.ShapeDtypeStruct((rows, width), jnp.bfloat16),
            jax.ShapeDtypeStruct((2, rows, width), jnp.bfloat16),
            jax.ShapeDtypeStruct((2, rows, width), jnp.bfloat16),
            jax.ShapeDtypeStruct((2, rows, width), jnp.float32),
            jax.ShapeDtypeStruct((2, n_sum * BLOCK, width), jnp.float32),
            jax.ShapeDtypeStruct((1,), jnp.int32),
        ],
        compiler_params=pltpu.CompilerParams(vmem_limit_bytes=40 * 1024 * 1024),
        cost_estimate=pl.CostEstimate(
            flops=heads * pairs * 10 * HDIM,
            bytes_accessed=heads * rows * HDIM * 32,
            transcendentals=heads * pairs,
        ),
    )(info, query, dout, kv2, kv1, kv0, kvs, after)


def on_device(query, key_in, value_in, dout, summary_offset):
    rows, width = query.shape
    me = lax.axis_index("ctx")
    n_ctx = lax.axis_size("ctx")
    n_tp = lax.axis_size("tp")
    n_sum = summary_offset.shape[0]
    groups = jnp.arange(n_sum, dtype=jnp.int32) * STRIDE + summary_offset
    owner = groups * BLOCK // rows
    local_start = groups * BLOCK - owner * rows
    distance = me - owner
    tile_distance = jnp.repeat(distance, BLOCK)[None, :, None]
    info = jnp.concatenate([me.astype(jnp.int32)[None], groups])
    odd = me % 2 == 1
    jumps = []
    reached = 2 * REACH
    while reached < n_ctx:
        jumps.append(reached)
        reached *= 2
    part = width // CHUNKS
    heads = part // HDIM

    stacked = []
    for chunk in range(CHUNKS):
        span = slice(chunk * part, (chunk + 1) * part)
        kv0 = jnp.stack([key_in[:, span], value_in[:, span]])
        stacked.append((kv0, shifted(kv0, "ctx", 2)))

    def gathered(kv0, kv2, here):
        kv1 = swapped(jnp.where(here % 2 == 1, kv2, kv0), "ctx")
        away = here - owner
        tiles = []
        for s in range(n_sum):
            at = (0, local_start[s], 0)
            size = (2, BLOCK, part)
            far = lax.dynamic_slice(kv2, at, size)
            own = lax.dynamic_slice(kv0, at, size)
            tiles.append(jnp.where(away[s] == 2, far, own))
        kvs = jnp.concatenate(tiles, axis=1)
        got = shifted(kvs, "ctx", 1)
        kvs = jnp.where((tile_distance == 1) | (tile_distance == 3), got, kvs)
        for jump in jumps:
            got = shifted(kvs, "ctx", jump)
            kvs = jnp.where((tile_distance >= jump) & (tile_distance < 2 * jump), got, kvs)
        return kv2, kv1, kv0, kvs

    def returned(p2, p1, p0, ps):
        for jump in reversed(jumps):
            got = shifted(ps.astype(jnp.bfloat16), "ctx", -jump).astype(jnp.float32)
            ps = jnp.where((tile_distance >= 0) & (tile_distance < jump), ps + got, ps)
        got = shifted(ps.astype(jnp.bfloat16), "ctx", -1).astype(jnp.float32)
        ps = jnp.where((tile_distance == 0) | (tile_distance == 2), ps + got, ps)

        def add_tile(array, s, away):
            at = (0, local_start[s], 0)
            piece = lax.dynamic_slice(array, at, (2, BLOCK, part)).astype(jnp.float32)
            term = jnp.where(distance[s] == away, ps[:, s * BLOCK : (s + 1) * BLOCK], 0.0)
            return lax.dynamic_update_slice(array, (piece + term).astype(array.dtype), at)

        for s in range(n_sum):
            p2 = add_tile(p2, s, 2)
            p0 = add_tile(p0, s, 0)
        near = swapped(p1, "ctx")
        wide = near.astype(jnp.float32)
        p2 = jnp.where(odd, p2.astype(jnp.float32) + wide, p2.astype(jnp.float32))
        far = shifted(p2.astype(jnp.bfloat16), "ctx", -2).astype(jnp.float32)
        total = (p0 + jnp.where(odd, 0.0, wide) + far).astype(jnp.bfloat16)
        return near, lax.all_to_all(total, "tp", split_axis=1, concat_axis=2, tiled=True)

    grads = []
    tokens = []
    returns = []
    for chunk in range(CHUNKS):
        here = tokens[chunk - 2][0] if chunk >= 2 else me
        after = returns[chunk - 2] if chunk >= 2 else summary_offset
        ready = gathered(*stacked[chunk], here)
        gq, p2, p1, p0, ps, token = attention(
            info, query, dout, *ready, after, chunk * heads, n_sum
        )
        tokens.append(token)
        moved_q = lax.all_to_all(gq, "tp", split_axis=0, concat_axis=1, tiled=True)
        near, moved_kv = returned(p2, p1, p0, ps)
        returns.append(near)
        grads.append((moved_q, moved_kv[0], moved_kv[1]))

    def joined(pieces):
        split = [piece.reshape(rows // n_tp, n_tp, part) for piece in pieces]
        return jnp.concatenate(split, axis=2).reshape(rows // n_tp, n_tp * width)

    return tuple(joined([grad[which] for grad in grads]) for which in range(3))


def solution(mesh):
    return jax.shard_map(
        on_device,
        mesh=mesh,
        in_specs=(P("ctx", "tp"), P("ctx", "tp"), P("ctx", "tp"), P("ctx", "tp"), P()),
        out_specs=(P(("ctx", "tp"), None), P(("ctx", "tp"), None), P(("ctx", "tp"), None)),
        check_vma=False,
    )
```
